32 devices in a mesh: dp: 4 (over y, x), tensor: 8 (over z, core).
Axes of the slice: x: 2, y: 2, z: 4, core: 2. Of those that a mesh axis runs over, the one named last changes fastest.
Arguments:
- hidden: bfloat16 [8192, 2048], P(('dp', 'tensor')), may hold values from -6 to 6
- norm_gain: float32 [2048], replicated, may hold values from 0.5 to 1.5
- head_weight: bfloat16 [2048, 102400], P('dp', 'tensor'), as said below
- token_ids: int32 [8192], P(('dp', 'tensor')), may hold values from 0 to 102399
- lengths: int32 [4, 4], P('dp'), may hold values from 1 to 512, 1024 in all within a row
Outputs:
- logprob: float32 [8192], P(('dp', 'tensor'))
- entropy: float32 [8192], P(('dp', 'tensor'))
The draws below stay inside these ranges and needn't reach their ends.
Inputs may be any that keep to these rules, and one draw needn't show every extreme that they name: Each index of dp has 4 lengths that sum to exactly 1024, and one of them equals 512. `head_weight`: head weights.
All inputs are finite; a program needn't handle non-finite values.
Results may differ from the reference program's by a relative error of at most 0.0045.
Values may be sent and summed in bfloat16 or wider, within the bound.
A program may use at most 256 MiB of HBM per device.

```python
import math
import jax
import jax.numpy as jnp
import numpy as np
from jax import lax

D = 2048
V = 102400
SEQ_DP = 4
SLOT = 512
ROWS = 8192
N_DP = 4


def column_draw(key, index):
    return jax.random.normal(jax.random.fold_in(jax.random.fold_in(key, 11), index), (D,), jnp.float32)


def hot_pairs(key):
    order = jax.random.permutation(jax.random.fold_in(key, 13), V)
    pairs = order[:16].reshape(8, 2).astype(jnp.int32)
    target = 110.0 + 30.0 * jnp.arange(8, dtype=jnp.float32)
    scales = target / (1.5 * math.sqrt(D))
    return (pairs, target, scales)


def draw_head_weight(key, part):
    columns = jax.vmap(lambda index: column_draw(key, index))(jnp.arange(V))
    columns = jnp.clip(columns, -6.0, 6.0)
    spread = jnp.exp(jax.random.uniform(jax.random.fold_in(key, 12), (V,), jnp.float32, math.log(0.6), math.log(4.0)))
    pairs, target, scales = hot_pairs(key)
    columns = columns.at[pairs[:, 1]].set(columns[pairs[:, 0]])
    spread = spread.at[pairs[:, 0]].set(scales)
    spread = spread.at[pairs[:, 1]].set(scales * (1.0 - 2.0 / target))
    full = columns * (1.5 / math.sqrt(D) * spread)[:, None]
    return full.T.astype(jnp.bfloat16)


def draw_hidden(key, part):
    base = jnp.clip(jax.random.normal(jax.random.fold_in(key, 21), (ROWS, D), jnp.float32), -6.0, 6.0)
    pairs, target, scales = hot_pairs(key)
    aligned = jax.vmap(lambda index: jnp.clip(column_draw(key, index), -6.0, 6.0))(pairs[:, 0])
    aligned = aligned / jnp.max(jnp.abs(aligned), axis=1, keepdims=True) * 3.0
    places = jnp.arange(8, dtype=jnp.int32) * SLOT
    base = base.at[places].set(aligned)
    return base.astype(jnp.bfloat16)


def draw_token_ids(key, part):
    ids = jax.random.randint(jax.random.fold_in(key, 31), (ROWS,), 0, V).astype(jnp.int32)
    pairs, target, scales = hot_pairs(key)
    pick = jax.random.randint(jax.random.fold_in(key, 32), (8,), 0, 2).astype(jnp.int32)
    hot_ids = jnp.where(pick == 0, pairs[:, 0], pairs[:, 1])
    places = jnp.arange(8, dtype=jnp.int32) * SLOT
    return ids.at[places].set(hot_ids)


def profile(number_of, total, reach, skew):
    portions = [(1 << 20) // math.isqrt(grade ** skew) + 1 for grade in range(2, number_of + 1)]
    rest, counts = total - reach - (number_of - 1), [1] * (number_of - 1)
    while rest > 0:
        candidates = [i for i in range(number_of - 1) if counts[i] < reach]
        mass, remaining = sum([portions[i] for i in candidates]), rest
        for i in candidates:
            more = min(reach - counts[i], max(1, remaining * portions[i] // mass), rest)
            counts[i] = counts[i] + more
            rest = rest - more
    return np.array([reach] + counts)


def uneven_parts(key, number_of, total, bound, lean):
    if number_of == 2:
        one = jax.random.randint(key, (), max(1, total - bound), min(bound, total - 1) + 1)
        return jnp.stack([one, total - one])
    sizes = jnp.asarray(profile(number_of, total, bound, lean), jnp.int32)
    pairs = (number_of - 1) // 2
    giver, sink = sizes[1:1 + 2 * pairs:2], sizes[2:2 + 2 * pairs:2]
    slack = jnp.minimum(giver - 1, bound - sink)
    shifted = jax.random.randint(jax.random.fold_in(key, 1), (pairs,), 0, 1 << 20) % (slack + 1)
    sizes = sizes.at[1:1 + 2 * pairs:2].set(giver - shifted).at[2:2 + 2 * pairs:2].set(sink + shifted)
    return sizes[jax.random.permutation(jax.random.fold_in(key, 2), number_of)]


def setup_inputs(seed: int = 0) -> dict:
    splits = jax.random.split(jax.random.key(seed), 6)
    return {
        "hidden": draw_hidden(jax.random.fold_in(splits[5], 71), 0),
        "norm_gain": jnp.clip(1.0 + 0.1 * jax.random.normal(splits[1], (D,), jnp.float32), 0.5, 1.5),
        "head_weight": draw_head_weight(jax.random.fold_in(splits[5], 71), 0),
        "token_ids": draw_token_ids(jax.random.fold_in(splits[5], 71), 0),
        "lengths": jax.vmap(lambda own: uneven_parts(own, SEQ_DP, 2 * SLOT, SLOT, 2))(jax.random.split(splits[4], N_DP)).reshape((N_DP, SEQ_DP)).astype(jnp.int32),
    }


def reference(hidden, norm_gain, head_weight, token_ids, lengths):
    wide = hidden.astype(jnp.float32)
    meansq = lax.optimization_barrier(jnp.mean(wide * wide, axis=-1, keepdims=True))
    normed = (wide * lax.rsqrt(meansq + 1e-06) * norm_gain).astype(jnp.bfloat16)
    rows = jnp.arange(ROWS, dtype=jnp.int32)
    seqnum = rows // SLOT
    within = rows % SLOT
    scored = within < lengths.reshape(-1)[seqnum]
    block = 256
    count = ROWS // block

    def one_block(args):
        normed_blk, ids_blk = args
        logits = jnp.dot(normed_blk, head_weight, preferred_element_type=jnp.float32)
        top = lax.optimization_barrier(jnp.max(logits, axis=1))
        expo = jnp.exp(logits - top[:, None])
        total = lax.optimization_barrier(jnp.sum(expo, axis=1))
        moment = lax.optimization_barrier(jnp.sum(expo * logits, axis=1))
        chosen = jnp.take_along_axis(logits, ids_blk[:, None].astype(jnp.int32), axis=1)[:, 0]
        lse = top + jnp.log(total)
        return (chosen - lse, lse - moment / total)
    lprob, entro = lax.map(one_block, (normed.reshape(count, block, D), token_ids.reshape(count, block)))
    zero = jnp.zeros((ROWS,), jnp.float32)
    return (jnp.where(scored, lprob.reshape(-1), zero), jnp.where(scored, entro.reshape(-1), zero))
```

```python
import functools

import jax
import jax.numpy as jnp
from jax import lax
from jax.experimental import pallas as pl
from jax.experimental.pallas import tpu as pltpu
from jax.sharding import PartitionSpec as P

SEQ_DP = 4
SLOT = 512
MESH = pl.DeviceIdType.MESH
TAIL = 128


def normalize(hidden, norm_gain):
    wide = hidden.astype(jnp.float32)
    meansq = jnp.mean(wide * wide, axis=-1, keepdims=True)
    return (wide * lax.rsqrt(meansq + 1e-06) * norm_gain).astype(jnp.bfloat16)


def plain_device(hidden, norm_gain, head_weight, token_ids, lengths):
    row_dev = hidden.shape[0]
    tensor_idx = lax.axis_index("tensor")
    normed = normalize(hidden, norm_gain)
    weight = lax.all_gather(head_weight, "dp", axis=0, tiled=True)
    vocab_dev = weight.shape[1]
    own_rows = tensor_idx * row_dev + jnp.arange(row_dev, dtype=jnp.int32)
    logits = jnp.dot(
        lax.all_gather(normed, "tensor", axis=0, tiled=True),
        weight,
        preferred_element_type=jnp.float32,
    )
    top = jnp.max(logits, axis=1)
    expo = jnp.exp(logits - top[:, None])
    total = jnp.sum(expo, axis=1)
    moment = jnp.sum(expo * logits, axis=1)
    ids = lax.all_gather(token_ids, "tensor", axis=0, tiled=True) - tensor_idx * vocab_dev
    hit = ids[:, None] == jnp.arange(vocab_dev, dtype=jnp.int32)[None, :]
    chosen = jnp.sum(jnp.where(hit, logits, 0.0), axis=1)
    seq_iota = jnp.arange(SEQ_DP, dtype=jnp.int32)
    onehot = (own_rows // SLOT)[:, None] == seq_iota[None, :]
    length_of = jnp.sum(jnp.where(onehot, lengths[0][None, :], 0), axis=1)
    scored = own_rows % SLOT < length_of
    top_all = lax.pmax(top, "tensor")
    rescale = jnp.exp(top - top_all)
    total_all, moment_all, chosen_all = lax.psum(
        (total * rescale, moment * rescale, chosen), "tensor"
    )
    return finish(
        scored, top_all[own_rows], total_all[own_rows], moment_all[own_rows], chosen_all[own_rows]
    )


def finish(scored, top, total, moment, chosen):
    safe_total = jnp.where(scored, total, 1.0)
    lse = top + jnp.log(safe_total)
    logprob = jnp.where(scored, chosen - lse, 0.0)
    entropy = jnp.where(scored, lse - moment / safe_total, 0.0)
    return (logprob, entropy)


def head_kernel(
    n_dp, n_z, chunks, x_ref, w_ref, out_ref,
    rows, weight, buf_a, buf_b, acc,
    plane_send, plane_recv, up_send, up_recv, down_send, down_recv,
    sib_send, sib_recv, w_send, w_recv, local_sem,
):
    dp = lax.axis_index("dp")
    t = lax.axis_index("tensor")
    z, core = t // 2, t % 2
    depth = w_ref.shape[0]
    vocab = weight.shape[1]
    share = x_ref.shape[0]
    width = weight.shape[0]
    block = n_dp * share

    barrier = pltpu.get_barrier_semaphore()
    for k in range(1, n_dp):
        pl.semaphore_signal(barrier, device_id=((dp + k) % n_dp, t), device_id_type=MESH)
    pl.semaphore_signal(barrier, device_id=(dp, z * 2 + 1 - core), device_id_type=MESH)

    @pl.when(z > 0)
    def _():
        pl.semaphore_signal(barrier, device_id=(dp, t - 2), device_id_type=MESH)

    @pl.when(z < n_z - 1)
    def _():
        pl.semaphore_signal(barrier, device_id=(dp, t + 2), device_id_type=MESH)

    ends = (z == 0).astype(jnp.int32) + (z == n_z - 1).astype(jnp.int32)
    pl.semaphore_wait(barrier, n_dp + 2 - ends)

    def remote(src, dst, send, recv, to):
        return pltpu.make_async_remote_copy(
            src_ref=src, dst_ref=dst, send_sem=send, recv_sem=recv,
            device_id=to, device_id_type=MESH,
        )

    def plane_copy(k, sender):
        return remote(
            x_ref,
            rows.at[z, core, pl.ds(pl.multiple_of(sender * share, share), share)],
            plane_send.at[k - 1], plane_recv.at[k - 1], ((dp + k) % n_dp, t),
        )

    for k in range(1, n_dp):
        plane_copy(k, dp).start()
    own_rows = pltpu.make_async_copy(
        x_ref, rows.at[z, core, pl.ds(pl.multiple_of(dp * share, share), share)], local_sem.at[0]
    )
    own_rows.start()

    def weight_copy(k, sender):
        peer = (dp + k) % n_dp
        return remote(
            w_ref.at[:, pl.ds(pl.multiple_of(peer * vocab, 128), vocab)],
            weight.at[pl.ds(pl.multiple_of(sender * depth, depth), depth)],
            w_send.at[k - 1], w_recv.at[k - 1], (peer, t),
        )

    for k in range(1, n_dp):
        weight_copy(k, dp).start()
    own_weight = pltpu.make_async_copy(
        w_ref.at[:, pl.ds(pl.multiple_of(dp * vocab, 128), vocab)],
        weight.at[pl.ds(pl.multiple_of(dp * depth, depth), depth)],
        local_sem.at[1],
    )
    own_weight.start()

    def up_copy(d):
        plane = z - d
        return remote(
            rows.at[plane, core], rows.at[plane, core],
            up_send.at[d], up_recv.at[d], (dp, t + 2),
        )

    def down_copy(d):
        plane = z + d
        return remote(
            rows.at[plane, core], rows.at[plane, core],
            down_send.at[d], down_recv.at[d], (dp, t - 2),
        )

    def sib_copy(plane, half):
        return remote(
            rows.at[plane, half], rows.at[plane, half],
            sib_send.at[plane], sib_recv.at[plane], (dp, z * 2 + 1 - core),
        )

    for k in range(1, n_dp):
        plane_copy(k, (dp - k + n_dp) % n_dp).wait_recv()
    own_rows.wait()

    @pl.when(z < n_z - 1)
    def _():
        up_copy(0).start()

    @pl.when(z > 0)
    def _():
        down_copy(0).start()

    sib_copy(z, core).start()

    for d in range(1, n_z):
        @pl.when(z >= d)
        def _():
            remote(
                rows.at[z - d, core], rows.at[z - d, core],
                up_send.at[d - 1], up_recv.at[d - 1], (dp, t),
            ).wait_recv()

            @pl.when(z < n_z - 1)
            def _():
                up_copy(d).start()

            sib_copy(z - d, core).start()

        @pl.when(z + d < n_z)
        def _():
            remote(
                rows.at[z + d, core], rows.at[z + d, core],
                down_send.at[d - 1], down_recv.at[d - 1], (dp, t),
            ).wait_recv()

            @pl.when(z > 0)
            def _():
                down_copy(d).start()

            sib_copy(z + d, core).start()

    for plane in range(n_z):
        sib_copy(plane, 1 - core).wait_recv()
    for k in range(1, n_dp):
        weight_copy(k, (dp - k + n_dp) % n_dp).wait_recv()
    own_weight.wait()

    first = t * (n_dp * vocab) + dp * vocab
    lane = lax.broadcasted_iota(jnp.int32, (1, 128), 1)
    strip = 16

    @pl.loop(0, n_z * 2)
    def _(step):
        plane, half = step // 2, step % 2
        tail = rows[plane, half, :, width:].astype(jnp.float32)
        place = jnp.where(
            lane == 0, 4096.0, jnp.where(lane == 1, 64.0, jnp.where(lane == 2, 1.0, 0.0))
        )
        ids = jnp.sum(tail * place, axis=1, keepdims=True).astype(jnp.int32)
        acc[0] = jnp.full((block, 128), -3e38, jnp.float32)
        acc[1] = jnp.zeros((block, 128), jnp.float32)
        acc[2] = jnp.zeros((block, 128), jnp.float32)
        acc[3] = jnp.zeros((block, 128), jnp.float32)
        shifted = ids - first - lane
        lhs = rows[plane, half, :, :width]
        at = 0
        for i, size in enumerate(chunks):
            buf = (buf_a, buf_b)[i % 2]
            buf[:, :size] = jnp.dot(
                lhs, weight[:, at : at + size], preferred_element_type=jnp.float32
            )
            for r in range(0, block, strip):
                part = slice(r, r + strip)
                groups = [buf[part, g : g + 128] for g in range(0, size, 128)]
                old = acc[0, part]
                top = old
                for g in groups:
                    top = jnp.maximum(top, g)
                scale = jnp.exp(old - top)
                total = acc[1, part] * scale
                moment = acc[2, part] * scale
                chosen = acc[3, part]
                for n, g in enumerate(groups):
                    e = jnp.exp(g - top)
                    total += e
                    moment += e * g
                    chosen += jnp.where(shifted[part] == at + n * 128, g, 0.0)
                acc[0, part] = top
                acc[1, part] = total
                acc[2, part] = moment
                acc[3, part] = chosen
            at += size
        top = jnp.max(acc[0], axis=1, keepdims=True)
        scale = jnp.exp(acc[0] - top)
        total = jnp.sum(acc[1] * scale, axis=1, keepdims=True)
        moment = jnp.sum(acc[2] * scale, axis=1, keepdims=True)
        chosen = jnp.sum(acc[3], axis=1, keepdims=True)
        packed = jnp.where(
            lane == 0, top, jnp.where(lane == 1, total, jnp.where(lane == 2, moment, chosen))
        )
        out_ref[step] = packed.T[:8]

    for k in range(1, n_dp):
        plane_copy(k, dp).wait_send()
        weight_copy(k, dp).wait_send()
    for plane in range(n_z):
        sib_copy(plane, core).wait_send()
    for d in range(n_z - 1):
        @pl.when((z >= d) & (z < n_z - 1))
        def _():
            up_copy(d).wait_send()

        @pl.when((z + d < n_z) & (z > 0))
        def _():
            down_copy(d).wait_send()


def head_stats(n_dp, n_z, mine, head_weight):
    share, wide = mine.shape
    depth, vocab_dev = head_weight.shape
    width, vocab, block = n_dp * depth, vocab_dev // n_dp, n_dp * share
    chunks = [512] * (vocab // 512) + ([vocab % 512] if vocab % 512 else [])
    dma = pltpu.SemaphoreType.DMA
    flops = 2 * n_z * 2 * block * width * vocab
    return pl.pallas_call(
        functools.partial(head_kernel, n_dp, n_z, chunks),
        out_shape=jax.ShapeDtypeStruct((n_z * 2, 8, block), jnp.float32),
        in_specs=[
            pl.BlockSpec(memory_space=pltpu.VMEM),
            pl.BlockSpec(memory_space=pl.ANY),
        ],
        out_specs=pl.BlockSpec(memory_space=pltpu.VMEM),
        scratch_shapes=[
            pltpu.VMEM((n_z, 2, block, wide), jnp.bfloat16),
            pltpu.VMEM((width, vocab), jnp.bfloat16),
            pltpu.VMEM((block, 512), jnp.float32),
            pltpu.VMEM((block, 512), jnp.float32),
            pltpu.VMEM((4, block, 128), jnp.float32),
            dma((n_dp - 1,)), dma((n_dp - 1,)),
            dma((n_z,)), dma((n_z,)), dma((n_z,)), dma((n_z,)),
            dma((n_z,)), dma((n_z,)),
            dma((n_dp - 1,)), dma((n_dp - 1,)),
            dma((2,)),
        ],
        compiler_params=pltpu.CompilerParams(
            collective_id=0, has_side_effects=True, vmem_limit_bytes=56 * 1024 * 1024
        ),
        cost_estimate=pl.CostEstimate(
            flops=flops, bytes_accessed=width * vocab * 2, transcendentals=n_z * 2 * block * vocab
        ),
    )(mine, head_weight)


def last_at_or_below(starts, value):
    return jnp.sum((value[:, None] >= starts[None, :]).astype(jnp.int32), axis=1) - 1


def pick(table, index):
    iota = jnp.arange(table.shape[0], dtype=jnp.int32)
    return jnp.sum(jnp.where(index[:, None] == iota[None, :], table[None, :], 0), axis=1)


def kernel_device(n_dp, n_tensor, hidden, norm_gain, head_weight, token_ids, lengths):
    row_dev = hidden.shape[0]
    n_z = n_tensor // 2
    t = lax.axis_index("tensor")
    z, core = t // 2, t % 2
    length = lengths[0]
    over = jnp.maximum(length - row_dev, 0)
    under = jnp.maximum(row_dev - length, 0)
    over_at = jnp.cumsum(over) - over
    under_at = jnp.cumsum(under) - under

    normed = normalize(hidden, norm_gain)
    lane = jnp.arange(TAIL, dtype=jnp.int32)[None, :]
    ids = token_ids[:, None]
    digits = jnp.where(
        lane == 0, ids // 4096, jnp.where(lane == 1, ids // 64 % 64, jnp.where(lane == 2, ids % 64, 0))
    )
    sent = jnp.concatenate([normed, digits.astype(jnp.bfloat16)], axis=1)

    share = row_dev // 2
    slot = t * share + jnp.arange(share, dtype=jnp.int32)
    place = slot % row_dev
    zs = jnp.full((share,), z, jnp.int32)
    own_len = pick(length, zs)
    extra = pick(under_at, zs) + place - own_len
    giver = last_at_or_below(over_at, extra)
    source = jnp.where(
        place < own_len,
        z * SLOT + place,
        giver * SLOT + row_dev + extra - pick(over_at, giver),
    )
    everyone = lax.all_gather(sent, "tensor", axis=0, tiled=True)
    chooser = source[:, None] == jnp.arange(n_tensor * row_dev, dtype=jnp.int32)[None, :]
    mine = jnp.dot(
        chooser.astype(jnp.bfloat16), everyone, preferred_element_type=jnp.float32
    ).astype(jnp.bfloat16)

    stats = head_stats(n_dp, n_z, mine, head_weight)[:, :4]
    stats = stats.reshape(n_tensor, 4, n_dp, share).transpose(2, 1, 0, 3).reshape(n_dp, 4, -1)

    def merge(parts):
        top = jnp.max(parts[:, 0], axis=0)
        scale = jnp.exp(parts[:, 0] - top)
        return jnp.stack([
            top,
            jnp.sum(parts[:, 1] * scale, axis=0),
            jnp.sum(parts[:, 2] * scale, axis=0),
            jnp.sum(parts[:, 3], axis=0),
        ])

    part = merge(lax.all_to_all(stats, "dp", 0, 0))
    full = merge(lax.all_gather(part, "tensor", axis=0))

    row = jnp.arange(row_dev, dtype=jnp.int32)
    zr = jnp.full((row_dev,), z, jnp.int32)
    extra = pick(over_at, zr) + row
    taker = last_at_or_below(under_at, extra)
    back = taker * row_dev + pick(length, taker) + extra - pick(under_at, taker)
    where = jnp.where(core == 0, z * row_dev + row, back)
    scored = core * row_dev + row < pick(length, zr)
    hit = where[:, None] == jnp.arange(n_tensor * share, dtype=jnp.int32)[None, :]
    own = [jnp.sum(jnp.where(hit, full[i][None, :], 0.0), axis=1) for i in range(4)]
    return finish(scored, *own)


def solution(mesh):
    n_dp, n_tensor = mesh.shape["dp"], mesh.shape["tensor"]

    def per_device(hidden, norm_gain, head_weight, token_ids, lengths):
        fits = (
            n_tensor == 2 * SEQ_DP
            and 2 * hidden.shape[0] == SLOT
            and head_weight.shape[1] % (128 * n_dp) == 0
        )
        if not fits:
            return plain_device(hidden, norm_gain, head_weight, token_ids, lengths)
        return kernel_device(n_dp, n_tensor, hidden, norm_gain, head_weight, token_ids, lengths)

    return jax.shard_map(
        per_device,
        mesh=mesh,
        in_specs=(
            P(("dp", "tensor"), None),
            P(),
            P("dp", "tensor"),
            P(("dp", "tensor")),
            P("dp", None),
        ),
        out_specs=(P(("dp", "tensor")), P(("dp", "tensor"))),
        check_vma=False,
    )
```

```python
import functools

import jax
import jax.numpy as jnp
from jax import lax
from jax.experimental import pallas as pl
from jax.experimental.pallas import tpu as pltpu
from jax.sharding import PartitionSpec as P

SEQ_DP = 4
SLOT = 512
MESH = pl.DeviceIdType.MESH
TAIL = 128


def normalize(hidden, norm_gain):
    wide = hidden.astype(jnp.float32)
    meansq = jnp.mean(wide * wide, axis=-1, keepdims=True)
    return (wide * lax.rsqrt(meansq + 1e-06) * norm_gain).astype(jnp.bfloat16)


def plain_device(hidden, norm_gain, head_weight, token_ids, lengths):
    row_dev = hidden.shape[0]
    tensor_idx = lax.axis_index("tensor")
    normed = normalize(hidden, norm_gain)
    weight = lax.all_gather(head_weight, "dp", axis=0, tiled=True)
    vocab_dev = weight.shape[1]
    own_rows = tensor_idx * row_dev + jnp.arange(row_dev, dtype=jnp.int32)
    logits = jnp.dot(
        lax.all_gather(normed, "tensor", axis=0, tiled=True),
        weight,
        preferred_element_type=jnp.float32,
    )
    top = jnp.max(logits, axis=1)
    expo = jnp.exp(logits - top[:, None])
    total = jnp.sum(expo, axis=1)
    moment = jnp.sum(expo * logits, axis=1)
    ids = lax.all_gather(token_ids, "tensor", axis=0, tiled=True) - tensor_idx * vocab_dev
    hit = ids[:, None] == jnp.arange(vocab_dev, dtype=jnp.int32)[None, :]
    chosen = jnp.sum(jnp.where(hit, logits, 0.0), axis=1)
    seq_iota = jnp.arange(SEQ_DP, dtype=jnp.int32)
    onehot = (own_rows // SLOT)[:, None] == seq_iota[None, :]
    length_of = jnp.sum(jnp.where(onehot, lengths[0][None, :], 0), axis=1)
    scored = own_rows % SLOT < length_of
    top_all = lax.pmax(top, "tensor")
    rescale = jnp.exp(top - top_all)
    total_all, moment_all, chosen_all = lax.psum(
        (total * rescale, moment * rescale, chosen), "tensor"
    )
    return finish(
        scored, top_all[own_rows], total_all[own_rows], moment_all[own_rows], chosen_all[own_rows]
    )


def finish(scored, top, total, moment, chosen):
    safe_total = jnp.where(scored, total, 1.0)
    lse = top + jnp.log(safe_total)
    logprob = jnp.where(scored, chosen - lse, 0.0)
    entropy = jnp.where(scored, lse - moment / safe_total, 0.0)
    return (logprob, entropy)


def head_kernel(
    n_dp, n_z, groups, x_ref, sel_ref, keep_ref, w_ref, out_ref,
    rows, weight, back, front, buf_a, buf_b, acc, stats, dp_parts, part, all_parts,
    plane_send, plane_recv, up_send, up_recv, down_send, down_recv,
    sib_send, sib_recv, w_send, w_recv, local_sem,
    bup_send, bup_recv, bdown_send, bdown_recv, bsib_send, bsib_recv,
    front_send, front_recv, sdp_send, sdp_recv, st_send, st_recv,
):
    dp = lax.axis_index("dp")
    t = lax.axis_index("tensor")
    z, core = t // 2, t % 2
    n_tensor = 2 * n_z
    depth = w_ref.shape[0]
    width, vocab = weight.shape
    share, wide = front.shape
    block = n_dp * share
    sibling = (dp, z * 2 + 1 - core)
    above, below = (dp, t + 2), (dp, t - 2)

    barrier = pltpu.get_barrier_semaphore()
    for k in range(1, n_dp):
        pl.semaphore_signal(barrier, device_id=((dp + k) % n_dp, t), device_id_type=MESH)
    for k in range(1, n_tensor):
        pl.semaphore_signal(barrier, device_id=(dp, (t + k) % n_tensor), device_id_type=MESH)
    pl.semaphore_wait(barrier, n_dp + n_tensor - 2)

    def remote(src, dst, send, recv, to):
        return pltpu.make_async_remote_copy(
            src_ref=src, dst_ref=dst, send_sem=send, recv_sem=recv,
            device_id=to, device_id_type=MESH,
        )

    def back_up(d):
        src = x_ref if d == 0 else back.at[z - d]
        return remote(src, back.at[z - d], bup_send.at[d], bup_recv.at[d], above)

    def back_down(d):
        src = x_ref if d == 0 else back.at[z + d]
        return remote(src, back.at[z + d], bdown_send.at[d], bdown_recv.at[d], below)

    def back_sib(plane):
        return remote(
            back.at[plane], back.at[plane], bsib_send.at[plane], bsib_recv.at[plane], sibling
        )

    front_copy = remote(x_ref.at[share : 2 * share], front, front_send, front_recv, sibling)
    own_front = pltpu.make_async_copy(x_ref.at[0:share], front, local_sem.at[0])

    @pl.when((core == 1) & (z < n_z - 1))
    def _():
        back_up(0).start()

    @pl.when((core == 1) & (z > 0))
    def _():
        back_down(0).start()

    @pl.when(core == 0)
    def _():
        front_copy.start()
        own_front.start()

    def weight_copy(g, k, sender):
        at, size = groups[g][0], sum(groups[g][1])
        peer = (dp + k) % n_dp
        return remote(
            w_ref.at[:, pl.ds(pl.multiple_of(peer * vocab + at, 128), size)],
            weight.at[pl.ds(pl.multiple_of(sender * depth, depth), depth), at : at + size],
            w_send.at[g, k - 1], w_recv.at[g, k - 1], (peer, t),
        )

    for g in range(2):
        for k in range(1, n_dp):
            weight_copy(g, k, dp).start()
    own_weight = pltpu.make_async_copy(
        w_ref.at[:, pl.ds(pl.multiple_of(dp * vocab, 128), vocab)],
        weight.at[pl.ds(pl.multiple_of(dp * depth, depth), depth)],
        local_sem.at[1],
    )
    own_weight.start()

    for d in range(1, n_z):
        @pl.when((core == 1) & (z >= d))
        def _():
            remote(
                back.at[z - d], back.at[z - d], bup_send.at[d - 1], bup_recv.at[d - 1], above
            ).wait_recv()

            @pl.when(z < n_z - 1)
            def _():
                back_up(d).start()

            back_sib(z - d).start()

        @pl.when((core == 1) & (z + d < n_z))
        def _():
            remote(
                back.at[z + d], back.at[z + d], bdown_send.at[d - 1], bdown_recv.at[d - 1], below
            ).wait_recv()

            @pl.when(z > 0)
            def _():
                back_down(d).start()

            back_sib(z + d).start()

    @pl.when(core == 0)
    def _():
        own_front.wait()
        for k in range(1, n_z):
            back_sib((z + k) % n_z).wait_recv()

    @pl.when(core == 1)
    def _():
        front_copy.wait_recv()

    own_at = pl.ds(pl.multiple_of(dp * share, share), share)
    for at in range(0, wide, 512):
        cols = slice(at, min(at + 512, wide))
        mine = front[:, cols].astype(jnp.float32) * keep_ref[:, :1]
        for k in range(1, n_z):
            plane = (z + k) % n_z
            mine += jnp.dot(
                sel_ref[plane], back[plane, :, cols], preferred_element_type=jnp.float32
            )
        rows[z, core, own_at, cols] = mine.astype(jnp.bfloat16)

    def plane_copy(k, sender):
        at = pl.ds(pl.multiple_of(sender * share, share), share)
        return remote(
            rows.at[z, core, at], rows.at[z, core, at],
            plane_send.at[k - 1], plane_recv.at[k - 1], ((dp + k) % n_dp, t),
        )

    for k in range(1, n_dp):
        plane_copy(k, dp).start()

    def up_copy(d):
        ref = rows.at[z - d, core]
        return remote(ref, ref, up_send.at[d], up_recv.at[d], above)

    def down_copy(d):
        ref = rows.at[z + d, core]
        return remote(ref, ref, down_send.at[d], down_recv.at[d], below)

    def sib_copy(plane, half):
        ref = rows.at[plane, half]
        return remote(ref, ref, sib_send.at[plane], sib_recv.at[plane], sibling)

    for k in range(1, n_dp):
        plane_copy(k, (dp - k + n_dp) % n_dp).wait_recv()

    @pl.when(z < n_z - 1)
    def _():
        up_copy(0).start()

    @pl.when(z > 0)
    def _():
        down_copy(0).start()

    sib_copy(z, core).start()

    def stage(d):
        @pl.when(z >= d)
        def _():
            ref = rows.at[z - d, core]
            remote(ref, ref, up_send.at[d - 1], up_recv.at[d - 1], above).wait_recv()

            @pl.when(z < n_z - 1)
            def _():
                up_copy(d).start()

            sib_copy(z - d, core).start()

        @pl.when(z + d < n_z)
        def _():
            ref = rows.at[z + d, core]
            remote(ref, ref, down_send.at[d - 1], down_recv.at[d - 1], below).wait_recv()

            @pl.when(z > 0)
            def _():
                down_copy(d).start()

            sib_copy(z + d, core).start()

    def wait_weights(g):
        for k in range(1, n_dp):
            weight_copy(g, k, (dp - k + n_dp) % n_dp).wait_recv()

    stage(1)
    own_weight.wait()
    wait_weights(0)

    first = t * (n_dp * vocab) + dp * vocab
    lane = lax.broadcasted_iota(jnp.int32, (1, 128), 1)
    strip = 16

    def multiply(plane, half, g):
        entry = plane * 2 + half
        tail = rows[plane, half, :, width:].astype(jnp.float32)
        place = jnp.where(
            lane == 0, 4096.0, jnp.where(lane == 1, 64.0, jnp.where(lane == 2, 1.0, 0.0))
        )
        ids = jnp.sum(tail * place, axis=1, keepdims=True).astype(jnp.int32)
        shifted = ids - first - lane
        lhs = rows[plane, half, :, :width]
        at, sizes = groups[g]
        for i, size in enumerate(sizes):
            buf = (buf_a, buf_b)[i % 2]
            buf[:, :size] = jnp.dot(
                lhs, weight[:, at : at + size], preferred_element_type=jnp.float32
            )
            for r in range(0, block, strip):
                rs = slice(r, r + strip)
                tiles = [buf[rs, c : c + 128] for c in range(0, size, 128)]
                old = acc[entry, 0, rs]
                top = old
                for tile in tiles:
                    top = jnp.maximum(top, tile)
                scale = jnp.exp(old - top)
                total = acc[entry, 1, rs] * scale
                moment = acc[entry, 2, rs] * scale
                chosen = acc[entry, 3, rs]
                for n, tile in enumerate(tiles):
                    e = jnp.exp(tile - top)
                    total += e
                    moment += e * tile
                    chosen += jnp.where(shifted[rs] == at + n * 128, tile, 0.0)
                acc[entry, 0, rs] = top
                acc[entry, 1, rs] = total
                acc[entry, 2, rs] = moment
                acc[entry, 3, rs] = chosen
            at += size

    near = n_z - 1

    @pl.loop(0, 4 * n_z)
    def _(it):
        unit, turn = it // 2, it % 2
        half = (core + turn) % 2
        second = ((unit >= near) & (unit < 2 * near)) | (unit == 2 * n_z - 1)
        order = jnp.where(unit < near, unit, jnp.where(unit < 2 * near, unit - near, near))
        plane = jnp.where(z < n_z // 2, order, n_z - 1 - order)
        entry = plane * 2 + half

        @pl.when(it == 4)
        def _():
            stage(2)

        @pl.when(it == 2 * near)
        def _():
            wait_weights(1)

        @pl.when(it == 4 * near)
        def _():
            stage(3)

        @pl.when(jnp.logical_not(second))
        def _():
            @pl.when(turn == 1)
            def _():
                sib_copy(plane, 1 - core).wait_recv()

            acc[entry, 0] = jnp.full((block, 128), -3e38, jnp.float32)
            for i in range(1, 4):
                acc[entry, i] = jnp.zeros((block, 128), jnp.float32)
            multiply(plane, half, 0)

        @pl.when(second)
        def _():
            multiply(plane, half, 1)
            lanes = acc[entry, 0]
            top = jnp.max(lanes, axis=1, keepdims=True)
            scale = jnp.exp(lanes - top)
            total = jnp.sum(acc[entry, 1] * scale, axis=1, keepdims=True)
            moment = jnp.sum(acc[entry, 2] * scale, axis=1, keepdims=True)
            chosen = jnp.sum(acc[entry, 3], axis=1, keepdims=True)
            packed = jnp.where(
                lane == 0, top, jnp.where(lane == 1, total, jnp.where(lane == 2, moment, chosen))
            )
            stats[entry] = packed.T[:8]

    def merge(parts, n):
        each = [parts[i] for i in range(n)]
        top = each[0][:, 0:1]
        for p in each[1:]:
            top = jnp.maximum(top, p[:, 0:1])
        total = moment = chosen = jnp.zeros_like(top)
        for p in each:
            scale = jnp.exp(p[:, 0:1] - top)
            total += p[:, 1:2] * scale
            moment += p[:, 2:3] * scale
            chosen += p[:, 3:4]
        return jnp.concatenate([top, total, moment, chosen] * 2, axis=1)

    def stats_dp(k, sender):
        peer = (dp + k) % n_dp
        return remote(
            stats.at[:, :, pl.ds(pl.multiple_of(peer * share, share), share)], dp_parts.at[sender],
            sdp_send.at[k - 1], sdp_recv.at[k - 1], (peer, t),
        )

    for k in range(1, n_dp):
        stats_dp(k, dp).start()
    own_stats = pltpu.make_async_copy(
        stats.at[:, :, pl.ds(pl.multiple_of(dp * share, share), share)], dp_parts.at[dp], local_sem.at[2]
    )
    own_stats.start()
    own_stats.wait()
    for k in range(1, n_dp):
        stats_dp(k, (dp - k + n_dp) % n_dp).wait_recv()
    part[...] = merge(dp_parts, n_dp)

    def stats_t(k, sender):
        return remote(
            part, all_parts.at[sender], st_send.at[k - 1], st_recv.at[k - 1],
            (dp, (t + k) % n_tensor),
        )

    for k in range(1, n_tensor):
        stats_t(k, t).start()
    all_parts[t] = part[...]
    for k in range(1, n_tensor):
        stats_t(k, (t - k + n_tensor) % n_tensor).wait_recv()
    out_ref[...] = merge(all_parts, n_tensor)

    for k in range(1, n_dp):
        plane_copy(k, dp).wait_send()
        stats_dp(k, dp).wait_send()
        for g in range(2):
            weight_copy(g, k, dp).wait_send()
    for k in range(1, n_tensor):
        stats_t(k, t).wait_send()
    for plane in range(n_z):
        sib_copy(plane, core).wait_send()

    @pl.when(core == 0)
    def _():
        front_copy.wait_send()

    @pl.when(core == 1)
    def _():
        for k in range(1, n_z):
            back_sib((z + k) % n_z).wait_send()

    for d in range(n_z - 1):
        @pl.when((z >= d) & (z < n_z - 1))
        def _():
            up_copy(d).wait_send()

            @pl.when(core == 1)
            def _():
                back_up(d).wait_send()

        @pl.when((z + d < n_z) & (z > 0))
        def _():
            down_copy(d).wait_send()

            @pl.when(core == 1)
            def _():
                back_down(d).wait_send()


def head_stats(n_dp, n_z, sent, select, keep, head_weight):
    wide = sent.shape[1]
    share = sent.shape[0] // 2
    depth, vocab_dev = head_weight.shape
    width, vocab, block = n_dp * depth, vocab_dev // n_dp, n_dp * share
    sizes = [512] * (vocab // 512) + ([vocab % 512] if vocab % 512 else [])
    cut = len(sizes) // 2
    groups = [(0, sizes[:cut]), (sum(sizes[:cut]), sizes[cut:])]
    dma = pltpu.SemaphoreType.DMA
    n_tensor = 2 * n_z
    f32, bf16 = jnp.float32, jnp.bfloat16
    vmem = pl.BlockSpec(memory_space=pltpu.VMEM)
    return pl.pallas_call(
        functools.partial(head_kernel, n_dp, n_z, groups),
        out_shape=jax.ShapeDtypeStruct((n_tensor, 8, share), f32),
        in_specs=[vmem, vmem, vmem, pl.BlockSpec(memory_space=pl.ANY)],
        out_specs=vmem,
        scratch_shapes=[
            pltpu.VMEM((n_z, 2, block, wide), bf16),
            pltpu.VMEM((width, vocab), bf16),
            pltpu.VMEM((n_z, 2 * share, wide), bf16),
            pltpu.VMEM((share, wide), bf16),
            pltpu.VMEM((block, 512), f32),
            pltpu.VMEM((block, 512), f32),
            pltpu.VMEM((n_tensor, 4, block, 128), f32),
            pltpu.VMEM((n_tensor, 8, block), f32),
            pltpu.VMEM((n_dp, n_tensor, 8, share), f32),
            pltpu.VMEM((n_tensor, 8, share), f32),
            pltpu.VMEM((n_tensor, n_tensor, 8, share), f32),
            dma((n_dp - 1,)), dma((n_dp - 1,)),
            dma((n_z,)), dma((n_z,)), dma((n_z,)), dma((n_z,)),
            dma((n_z,)), dma((n_z,)),
            dma((2, n_dp - 1)), dma((2, n_dp - 1)),
            dma((3,)),
            dma((n_z,)), dma((n_z,)), dma((n_z,)), dma((n_z,)),
            dma((n_z,)), dma((n_z,)),
            dma, dma,
            dma((n_dp - 1,)), dma((n_dp - 1,)),
            dma((n_tensor - 1,)), dma((n_tensor - 1,)),
        ],
        compiler_params=pltpu.CompilerParams(
            collective_id=0, has_side_effects=True, vmem_limit_bytes=60 * 1024 * 1024
        ),
        cost_estimate=pl.CostEstimate(
            flops=2 * n_tensor * block * width * vocab,
            bytes_accessed=width * vocab * 2,
            transcendentals=n_tensor * block * vocab,
        ),
    )(sent, select, keep, head_weight)


def last_at_or_below(starts, value):
    return jnp.sum((value[:, None] >= starts[None, :]).astype(jnp.int32), axis=1) - 1


def pick(table, index):
    iota = jnp.arange(table.shape[0], dtype=jnp.int32)
    return jnp.sum(jnp.where(index[:, None] == iota[None, :], table[None, :], 0), axis=1)


def kernel_device(n_dp, n_tensor, hidden, norm_gain, head_weight, token_ids, lengths):
    row_dev = hidden.shape[0]
    n_z = n_tensor // 2
    t = lax.axis_index("tensor")
    z, core = t // 2, t % 2
    length = lengths[0]
    over = jnp.maximum(length - row_dev, 0)
    under = jnp.maximum(row_dev - length, 0)
    over_at = jnp.cumsum(over) - over
    under_at = jnp.cumsum(under) - under

    normed = normalize(hidden, norm_gain)
    lane = jnp.arange(TAIL, dtype=jnp.int32)[None, :]
    ids = token_ids[:, None]
    digits = jnp.where(
        lane == 0, ids // 4096, jnp.where(lane == 1, ids // 64 % 64, jnp.where(lane == 2, ids % 64, 0))
    )
    sent = jnp.concatenate([normed, digits.astype(jnp.bfloat16)], axis=1)

    share = row_dev // 2
    slot = t * share + jnp.arange(share, dtype=jnp.int32)
    place = slot % row_dev
    zs = jnp.full((share,), z, jnp.int32)
    own_len = pick(length, zs)
    extra = pick(under_at, zs) + place - own_len
    giver = last_at_or_below(over_at, extra)
    from_back = extra - pick(over_at, giver)
    filled = (place >= own_len)[None, :] & (giver[None, :] == jnp.arange(n_z, dtype=jnp.int32)[:, None])
    row_iota = jnp.arange(row_dev, dtype=jnp.int32)
    select = filled[:, :, None] & (from_back[:, None] == row_iota[None, :])[None]
    select = select.astype(jnp.bfloat16)
    keep = jnp.broadcast_to((place < own_len)[:, None], (share, 128)).astype(jnp.float32)
    full = head_stats(n_dp, n_z, sent, select, keep, head_weight)
    full = full[:, :4].transpose(1, 0, 2).reshape(4, -1)

    row = jnp.arange(row_dev, dtype=jnp.int32)
    zr = jnp.full((row_dev,), z, jnp.int32)
    extra = pick(over_at, zr) + row
    taker = last_at_or_below(under_at, extra)
    back = taker * row_dev + pick(length, taker) + extra - pick(under_at, taker)
    where = jnp.where(core == 0, z * row_dev + row, back)
    scored = core * row_dev + row < pick(length, zr)
    hit = where[:, None] == jnp.arange(n_tensor * share, dtype=jnp.int32)[None, :]
    own = [jnp.sum(jnp.where(hit, full[i][None, :], 0.0), axis=1) for i in range(4)]
    return finish(scored, *own)


def solution(mesh):
    n_dp, n_tensor = mesh.shape["dp"], mesh.shape["tensor"]

    def per_device(hidden, norm_gain, head_weight, token_ids, lengths):
        fits = (
            n_tensor == 2 * SEQ_DP
            and 2 * hidden.shape[0] == SLOT
            and head_weight.shape[1] % (128 * n_dp) == 0
        )
        if not fits:
            return plain_device(hidden, norm_gain, head_weight, token_ids, lengths)
        return kernel_device(n_dp, n_tensor, hidden, norm_gain, head_weight, token_ids, lengths)

    return jax.shard_map(
        per_device,
        mesh=mesh,
        in_specs=(
            P(("dp", "tensor"), None),
            P(),
            P("dp", "tensor"),
            P(("dp", "tensor")),
            P("dp", None),
        ),
        out_specs=(P(("dp", "tensor")), P(("dp", "tensor"))),
        check_vma=False,
    )
```

```python
import functools

import jax
import jax.numpy as jnp
from jax import lax
from jax.experimental import pallas as pl
from jax.experimental.pallas import tpu as pltpu
from jax.sharding import PartitionSpec as P

SEQ_DP = 4
SLOT = 512
MESH = pl.DeviceIdType.MESH
TAIL = 128


def normalize(hidden, norm_gain):
    wide = hidden.astype(jnp.float32)
    meansq = jnp.mean(wide * wide, axis=-1, keepdims=True)
    return (wide * lax.rsqrt(meansq + 1e-06) * norm_gain).astype(jnp.bfloat16)


def plain_device(hidden, norm_gain, head_weight, token_ids, lengths):
    row_dev = hidden.shape[0]
    tensor_idx = lax.axis_index("tensor")
    normed = normalize(hidden, norm_gain)
    weight = lax.all_gather(head_weight, "dp", axis=0, tiled=True)
    vocab_dev = weight.shape[1]
    own_rows = tensor_idx * row_dev + jnp.arange(row_dev, dtype=jnp.int32)
    logits = jnp.dot(
        lax.all_gather(normed, "tensor", axis=0, tiled=True),
        weight,
        preferred_element_type=jnp.float32,
    )
    top = jnp.max(logits, axis=1)
    expo = jnp.exp(logits - top[:, None])
    total = jnp.sum(expo, axis=1)
    moment = jnp.sum(expo * logits, axis=1)
    ids = lax.all_gather(token_ids, "tensor", axis=0, tiled=True) - tensor_idx * vocab_dev
    hit = ids[:, None] == jnp.arange(vocab_dev, dtype=jnp.int32)[None, :]
    chosen = jnp.sum(jnp.where(hit, logits, 0.0), axis=1)
    seq_iota = jnp.arange(SEQ_DP, dtype=jnp.int32)
    onehot = (own_rows // SLOT)[:, None] == seq_iota[None, :]
    length_of = jnp.sum(jnp.where(onehot, lengths[0][None, :], 0), axis=1)
    scored = own_rows % SLOT < length_of
    top_all = lax.pmax(top, "tensor")
    rescale = jnp.exp(top - top_all)
    total_all, moment_all, chosen_all = lax.psum(
        (total * rescale, moment * rescale, chosen), "tensor"
    )
    return finish(
        scored, top_all[own_rows], total_all[own_rows], moment_all[own_rows], chosen_all[own_rows]
    )


def finish(scored, top, total, moment, chosen):
    safe_total = jnp.where(scored, total, 1.0)
    lse = top + jnp.log(safe_total)
    logprob = jnp.where(scored, chosen - lse, 0.0)
    entropy = jnp.where(scored, lse - moment / safe_total, 0.0)
    return (logprob, entropy)


def head_kernel(
    n_dp, n_z, groups, x_ref, sel_ref, keep_ref, w_ref, out_ref,
    rows, weight, back, front, buf_a, buf_b, acc, stats, dp_parts, part, all_parts,
    plane_send, plane_recv, up_send, up_recv, down_send, down_recv,
    sib_send, sib_recv, w_send, w_recv, local_sem,
    bup_send, bup_recv, bdown_send, bdown_recv, bsib_send, bsib_recv,
    front_send, front_recv, sdp_send, sdp_recv, st_send, st_recv,
):
    dp = lax.axis_index("dp")
    t = lax.axis_index("tensor")
    z, core = t // 2, t % 2
    n_tensor = 2 * n_z
    depth = w_ref.shape[0]
    width, vocab = weight.shape
    share, wide = front.shape
    block = n_dp * share
    sibling = (dp, z * 2 + 1 - core)
    above, below = (dp, t + 2), (dp, t - 2)

    barrier = pltpu.get_barrier_semaphore()
    for k in range(1, n_dp):
        pl.semaphore_signal(barrier, device_id=((dp + k) % n_dp, t), device_id_type=MESH)
    for k in range(1, n_tensor):
        pl.semaphore_signal(barrier, device_id=(dp, (t + k) % n_tensor), device_id_type=MESH)
    pl.semaphore_wait(barrier, n_dp + n_tensor - 2)

    def remote(src, dst, send, recv, to):
        return pltpu.make_async_remote_copy(
            src_ref=src, dst_ref=dst, send_sem=send, recv_sem=recv,
            device_id=to, device_id_type=MESH,
        )

    def back_up(d):
        src = x_ref if d == 0 else back.at[z - d]
        return remote(src, back.at[z - d], bup_send.at[d], bup_recv.at[d], above)

    def back_down(d):
        src = x_ref if d == 0 else back.at[z + d]
        return remote(src, back.at[z + d], bdown_send.at[d], bdown_recv.at[d], below)

    def back_sib(plane):
        return remote(
            back.at[plane], back.at[plane], bsib_send.at[plane], bsib_recv.at[plane], sibling
        )

    front_copy = remote(x_ref.at[share : 2 * share], front, front_send, front_recv, sibling)
    own_front = pltpu.make_async_copy(x_ref.at[0:share], front, local_sem.at[0])

    @pl.when((core == 1) & (z < n_z - 1))
    def _():
        back_up(0).start()

    @pl.when((core == 1) & (z > 0))
    def _():
        back_down(0).start()

    @pl.when(core == 0)
    def _():
        front_copy.start()
        own_front.start()

    def weight_copy(g, k, sender):
        at, size = groups[g][0], sum(groups[g][1])
        peer = (dp + k) % n_dp
        return remote(
            w_ref.at[:, pl.ds(pl.multiple_of(peer * vocab + at, 128), size)],
            weight.at[pl.ds(pl.multiple_of(sender * depth, depth), depth), at : at + size],
            w_send.at[g, k - 1], w_recv.at[g, k - 1], (peer, t),
        )

    for k in range(1, n_dp):
        weight_copy(0, k, dp).start()
    own_weight = pltpu.make_async_copy(
        w_ref.at[:, pl.ds(pl.multiple_of(dp * vocab, 128), vocab)],
        weight.at[pl.ds(pl.multiple_of(dp * depth, depth), depth)],
        local_sem.at[1],
    )
    own_weight.start()

    for d in range(1, n_z):
        @pl.when((core == 1) & (z >= d))
        def _():
            remote(
                back.at[z - d], back.at[z - d], bup_send.at[d - 1], bup_recv.at[d - 1], above
            ).wait_recv()

            @pl.when(z < n_z - 1)
            def _():
                back_up(d).start()

            back_sib(z - d).start()

        @pl.when((core == 1) & (z + d < n_z))
        def _():
            remote(
                back.at[z + d], back.at[z + d], bdown_send.at[d - 1], bdown_recv.at[d - 1], below
            ).wait_recv()

            @pl.when(z > 0)
            def _():
                back_down(d).start()

            back_sib(z + d).start()

    @pl.when(core == 0)
    def _():
        own_front.wait()
        for k in range(1, n_z):
            back_sib((z + k) % n_z).wait_recv()

    @pl.when(core == 1)
    def _():
        front_copy.wait_recv()

    own_at = pl.ds(pl.multiple_of(dp * share, share), share)
    for at in range(0, wide, 512):
        cols = slice(at, min(at + 512, wide))
        mine = front[:, cols].astype(jnp.float32) * keep_ref[:, :1]
        for k in range(1, n_z):
            plane = (z + k) % n_z
            mine += jnp.dot(
                sel_ref[plane], back[plane, :, cols], preferred_element_type=jnp.float32
            )
        rows[z, core, own_at, cols] = mine.astype(jnp.bfloat16)

    def plane_copy(k, sender):
        at = pl.ds(pl.multiple_of(sender * share, share), share)
        return remote(
            rows.at[z, core, at], rows.at[z, core, at],
            plane_send.at[k - 1], plane_recv.at[k - 1], ((dp + k) % n_dp, t),
        )

    for k in range(1, n_dp):
        plane_copy(k, dp).start()
    for g in range(1, len(groups)):
        for k in range(1, n_dp):
            weight_copy(g, k, dp).start()

    def share_of(plane, k):
        at = pl.multiple_of((dp - k + n_dp) % n_dp * share, share)
        return rows.at[plane, core, pl.ds(at, share)]

    def up_copy(d, k, plane):
        ref = share_of(plane, k)
        return remote(ref, ref, up_send.at[d, k], up_recv.at[d, k], above)

    def down_copy(d, k, plane):
        ref = share_of(plane, k)
        return remote(ref, ref, down_send.at[d, k], down_recv.at[d, k], below)

    def sib_copy(plane, half):
        ref = rows.at[plane, half]
        return remote(ref, ref, sib_send.at[plane], sib_recv.at[plane], sibling)

    for k in range(n_dp):
        if k:
            plane_copy(k, (dp - k + n_dp) % n_dp).wait_recv()

        @pl.when(z < n_z - 1)
        def _():
            up_copy(0, k, z).start()

        @pl.when(z > 0)
        def _():
            down_copy(0, k, z).start()

    sib_copy(z, core).start()

    def stage(d):
        for k in range(n_dp):
            @pl.when(z >= d)
            def _():
                up_copy(d - 1, k, z - d).wait_recv()

                @pl.when(z < n_z - 1)
                def _():
                    up_copy(d, k, z - d).start()

            @pl.when(z + d < n_z)
            def _():
                down_copy(d - 1, k, z + d).wait_recv()

                @pl.when(z > 0)
                def _():
                    down_copy(d, k, z + d).start()

        @pl.when(z >= d)
        def _():
            sib_copy(z - d, core).start()

        @pl.when(z + d < n_z)
        def _():
            sib_copy(z + d, core).start()

    def wait_weights(g):
        for k in range(1, n_dp):
            weight_copy(g, k, (dp - k + n_dp) % n_dp).wait_recv()

    stage(1)
    own_weight.wait()
    wait_weights(0)

    first = t * (n_dp * vocab) + dp * vocab
    lane = lax.broadcasted_iota(jnp.int32, (1, 128), 1)
    strip = 16

    def multiply(plane, half, g):
        entry = plane * 2 + half
        tail = rows[plane, half, :, width:].astype(jnp.float32)
        place = jnp.where(
            lane == 0, 4096.0, jnp.where(lane == 1, 64.0, jnp.where(lane == 2, 1.0, 0.0))
        )
        ids = jnp.sum(tail * place, axis=1, keepdims=True).astype(jnp.int32)
        shifted = ids - first - lane
        lhs = rows[plane, half, :, :width]
        at, sizes = groups[g]
        for i, size in enumerate(sizes):
            buf = (buf_a, buf_b)[i % 2]
            buf[:, :size] = jnp.dot(
                lhs, weight[:, at : at + size], preferred_element_type=jnp.float32
            )
            for r in range(0, block, strip):
                rs = slice(r, r + strip)
                tiles = [buf[rs, c : c + 128] for c in range(0, size, 128)]
                old = acc[entry, 0, rs]
                top = old
                for tile in tiles:
                    top = jnp.maximum(top, tile)
                scale = jnp.exp(old - top)
                total = acc[entry, 1, rs] * scale
                moment = acc[entry, 2, rs] * scale
                chosen = acc[entry, 3, rs]
                for n, tile in enumerate(tiles):
                    e = jnp.exp(tile - top)
                    total += e
                    moment += e * tile
                    chosen += jnp.where(shifted[rs] == at + n * 128, tile, 0.0)
                acc[entry, 0, rs] = top
                acc[entry, 1, rs] = total
                acc[entry, 2, rs] = moment
                acc[entry, 3, rs] = chosen
            at += size

    near = n_z - 1
    last = len(groups) - 1

    @pl.loop(0, 2 * len(groups) * n_z)
    def _(it):
        unit, turn = it // 2, it % 2
        half = (core + turn) % 2
        far = unit >= near * len(groups)
        group = jnp.where(far, unit - near * len(groups), unit // near)
        order = jnp.where(far, near, unit % near)
        plane = jnp.where(z < n_z // 2, order, n_z - 1 - order)
        entry = plane * 2 + half

        @pl.when(it == 4)
        def _():
            stage(2)

        for g in range(1, len(groups)):
            @pl.when(it == 2 * near * g)
            def _():
                wait_weights(g)

        @pl.when(it == 2 * near * len(groups))
        def _():
            stage(3)

        @pl.when(group == 0)
        def _():
            @pl.when(turn == 1)
            def _():
                sib_copy(plane, 1 - core).wait_recv()

            acc[entry, 0] = jnp.full((block, 128), -3e38, jnp.float32)
            for i in range(1, 4):
                acc[entry, i] = jnp.zeros((block, 128), jnp.float32)

        for g in range(len(groups)):
            @pl.when(group == g)
            def _():
                multiply(plane, half, g)

        @pl.when(group == last)
        def _():
            lanes = acc[entry, 0]
            top = jnp.max(lanes, axis=1, keepdims=True)
            scale = jnp.exp(lanes - top)
            total = jnp.sum(acc[entry, 1] * scale, axis=1, keepdims=True)
            moment = jnp.sum(acc[entry, 2] * scale, axis=1, keepdims=True)
            chosen = jnp.sum(acc[entry, 3], axis=1, keepdims=True)
            packed = jnp.where(
                lane == 0, top, jnp.where(lane == 1, total, jnp.where(lane == 2, moment, chosen))
            )
            stats[entry] = packed.T[:8]

    def merge(parts, n):
        each = [parts[i] for i in range(n)]
        top = each[0][:, 0:1]
        for p in each[1:]:
            top = jnp.maximum(top, p[:, 0:1])
        total = moment = chosen = jnp.zeros_like(top)
        for p in each:
            scale = jnp.exp(p[:, 0:1] - top)
            total += p[:, 1:2] * scale
            moment += p[:, 2:3] * scale
            chosen += p[:, 3:4]
        return jnp.concatenate([top, total, moment, chosen] * 2, axis=1)

    def stats_dp(k, sender):
        peer = (dp + k) % n_dp
        return remote(
            stats.at[:, :, pl.ds(pl.multiple_of(peer * share, share), share)], dp_parts.at[sender],
            sdp_send.at[k - 1], sdp_recv.at[k - 1], (peer, t),
        )

    for k in range(1, n_dp):
        stats_dp(k, dp).start()
    own_stats = pltpu.make_async_copy(
        stats.at[:, :, pl.ds(pl.multiple_of(dp * share, share), share)], dp_parts.at[dp], local_sem.at[2]
    )
    own_stats.start()
    own_stats.wait()
    for k in range(1, n_dp):
        stats_dp(k, (dp - k + n_dp) % n_dp).wait_recv()
    part[...] = merge(dp_parts, n_dp)

    def stats_t(k, sender):
        return remote(
            part, all_parts.at[sender], st_send.at[k - 1], st_recv.at[k - 1],
            (dp, (t + k) % n_tensor),
        )

    for k in range(1, n_tensor):
        stats_t(k, t).start()
    all_parts[t] = part[...]
    for k in range(1, n_tensor):
        stats_t(k, (t - k + n_tensor) % n_tensor).wait_recv()
    out_ref[...] = merge(all_parts, n_tensor)

    for k in range(1, n_dp):
        plane_copy(k, dp).wait_send()
        stats_dp(k, dp).wait_send()
        for g in range(len(groups)):
            weight_copy(g, k, dp).wait_send()
    for k in range(1, n_tensor):
        stats_t(k, t).wait_send()
    for plane in range(n_z):
        sib_copy(plane, core).wait_send()

    @pl.when(core == 0)
    def _():
        front_copy.wait_send()

    @pl.when(core == 1)
    def _():
        for k in range(1, n_z):
            back_sib((z + k) % n_z).wait_send()

    for d in range(n_z - 1):
        @pl.when((z >= d) & (z < n_z - 1))
        def _():
            for k in range(n_dp):
                up_copy(d, k, z - d).wait_send()

            @pl.when(core == 1)
            def _():
                back_up(d).wait_send()

        @pl.when((z + d < n_z) & (z > 0))
        def _():
            for k in range(n_dp):
                down_copy(d, k, z + d).wait_send()

            @pl.when(core == 1)
            def _():
                back_down(d).wait_send()


def split_columns(vocab):
    first = vocab * 6 // 25 // 128 * 128
    second = vocab * 12 // 25 // 128 * 128
    return [first, second, vocab - first - second]


def head_stats(n_dp, n_z, sent, select, keep, head_weight):
    wide = sent.shape[1]
    share = sent.shape[0] // 2
    depth, vocab_dev = head_weight.shape
    width, vocab, block = n_dp * depth, vocab_dev // n_dp, n_dp * share
    groups, at = [], 0
    for part in split_columns(vocab):
        sizes = [min(512, part - done) for done in range(0, part, 512)]
        groups.append((at, sizes))
        at += part
    dma = pltpu.SemaphoreType.DMA
    n_tensor = 2 * n_z
    f32, bf16 = jnp.float32, jnp.bfloat16
    vmem = pl.BlockSpec(memory_space=pltpu.VMEM)
    return pl.pallas_call(
        functools.partial(head_kernel, n_dp, n_z, groups),
        out_shape=jax.ShapeDtypeStruct((n_tensor, 8, share), f32),
        in_specs=[vmem, vmem, vmem, pl.BlockSpec(memory_space=pl.ANY)],
        out_specs=vmem,
        scratch_shapes=[
            pltpu.VMEM((n_z, 2, block, wide), bf16),
            pltpu.VMEM((width, vocab), bf16),
            pltpu.VMEM((n_z, 2 * share, wide), bf16),
            pltpu.VMEM((share, wide), bf16),
            pltpu.VMEM((block, 512), f32),
            pltpu.VMEM((block, 512), f32),
            pltpu.VMEM((n_tensor, 4, block, 128), f32),
            pltpu.VMEM((n_tensor, 8, block), f32),
            pltpu.VMEM((n_dp, n_tensor, 8, share), f32),
            pltpu.VMEM((n_tensor, 8, share), f32),
            pltpu.VMEM((n_tensor, n_tensor, 8, share), f32),
            dma((n_dp - 1,)), dma((n_dp - 1,)),
            dma((n_z, n_dp)), dma((n_z, n_dp)), dma((n_z, n_dp)), dma((n_z, n_dp)),
            dma((n_z,)), dma((n_z,)),
            dma((len(groups), n_dp - 1)), dma((len(groups), n_dp - 1)),
            dma((3,)),
            dma((n_z,)), dma((n_z,)), dma((n_z,)), dma((n_z,)),
            dma((n_z,)), dma((n_z,)),
            dma, dma,
            dma((n_dp - 1,)), dma((n_dp - 1,)),
            dma((n_tensor - 1,)), dma((n_tensor - 1,)),
        ],
        compiler_params=pltpu.CompilerParams(
            collective_id=0, has_side_effects=True, vmem_limit_bytes=60 * 1024 * 1024
        ),
        cost_estimate=pl.CostEstimate(
            flops=2 * n_tensor * block * width * vocab,
            bytes_accessed=width * vocab * 2,
            transcendentals=n_tensor * block * vocab,
        ),
    )(sent, select, keep, head_weight)


def last_at_or_below(starts, value):
    return jnp.sum((value[:, None] >= starts[None, :]).astype(jnp.int32), axis=1) - 1


def pick(table, index):
    iota = jnp.arange(table.shape[0], dtype=jnp.int32)
    return jnp.sum(jnp.where(index[:, None] == iota[None, :], table[None, :], 0), axis=1)


def kernel_device(n_dp, n_tensor, hidden, norm_gain, head_weight, token_ids, lengths):
    row_dev = hidden.shape[0]
    n_z = n_tensor // 2
    t = lax.axis_index("tensor")
    z, core = t // 2, t % 2
    length = lengths[0]
    over = jnp.maximum(length - row_dev, 0)
    under = jnp.maximum(row_dev - length, 0)
    over_at = jnp.cumsum(over) - over
    under_at = jnp.cumsum(under) - under

    normed = normalize(hidden, norm_gain)
    lane = jnp.arange(TAIL, dtype=jnp.int32)[None, :]
    ids = token_ids[:, None]
    digits = jnp.where(
        lane == 0, ids // 4096, jnp.where(lane == 1, ids // 64 % 64, jnp.where(lane == 2, ids % 64, 0))
    )
    sent = jnp.concatenate([normed, digits.astype(jnp.bfloat16)], axis=1)

    share = row_dev // 2
    slot = t * share + jnp.arange(share, dtype=jnp.int32)
    place = slot % row_dev
    zs = jnp.full((share,), z, jnp.int32)
    own_len = pick(length, zs)
    extra = pick(under_at, zs) + place - own_len
    giver = last_at_or_below(over_at, extra)
    from_back = extra - pick(over_at, giver)
    filled = (place >= own_len)[None, :] & (giver[None, :] == jnp.arange(n_z, dtype=jnp.int32)[:, None])
    row_iota = jnp.arange(row_dev, dtype=jnp.int32)
    select = filled[:, :, None] & (from_back[:, None] == row_iota[None, :])[None]
    select = select.astype(jnp.bfloat16)
    keep = jnp.broadcast_to((place < own_len)[:, None], (share, 128)).astype(jnp.float32)
    full = head_stats(n_dp, n_z, sent, select, keep, head_weight)
    full = full[:, :4].transpose(1, 0, 2).reshape(4, -1)

    row = jnp.arange(row_dev, dtype=jnp.int32)
    zr = jnp.full((row_dev,), z, jnp.int32)
    extra = pick(over_at, zr) + row
    taker = last_at_or_below(under_at, extra)
    back = taker * row_dev + pick(length, taker) + extra - pick(under_at, taker)
    where = jnp.where(core == 0, z * row_dev + row, back)
    scored = core * row_dev + row < pick(length, zr)
    hit = where[:, None] == jnp.arange(n_tensor * share, dtype=jnp.int32)[None, :]
    own = [jnp.sum(jnp.where(hit, full[i][None, :], 0.0), axis=1) for i in range(4)]
    return finish(scored, *own)


def solution(mesh):
    n_dp, n_tensor = mesh.shape["dp"], mesh.shape["tensor"]

    def per_device(hidden, norm_gain, head_weight, token_ids, lengths):
        fits = (
            n_tensor == 2 * SEQ_DP
            and 2 * hidden.shape[0] == SLOT
            and head_weight.shape[1] % (128 * n_dp) == 0
        )
        if not fits:
            return plain_device(hidden, norm_gain, head_weight, token_ids, lengths)
        return kernel_device(n_dp, n_tensor, hidden, norm_gain, head_weight, token_ids, lengths)

    return jax.shard_map(
        per_device,
        mesh=mesh,
        in_specs=(
            P(("dp", "tensor"), None),
            P(),
            P("dp", "tensor"),
            P(("dp", "tensor")),
            P("dp", None),
        ),
        out_specs=(P(("dp", "tensor")), P(("dp", "tensor"))),
        check_vma=False,
    )
```

```python
import functools

import jax
import jax.numpy as jnp
from jax import lax
from jax.experimental import pallas as pl
from jax.experimental.pallas import tpu as pltpu
from jax.sharding import PartitionSpec as P

SEQ_DP = 4
SLOT = 512
MESH = pl.DeviceIdType.MESH
TAIL = 128


def normalize(hidden, norm_gain):
    wide = hidden.astype(jnp.float32)
    meansq = jnp.mean(wide * wide, axis=-1, keepdims=True)
    return (wide * lax.rsqrt(meansq + 1e-06) * norm_gain).astype(jnp.bfloat16)


def plain_device(hidden, norm_gain, head_weight, token_ids, lengths):
    row_dev = hidden.shape[0]
    tensor_idx = lax.axis_index("tensor")
    normed = normalize(hidden, norm_gain)
    weight = lax.all_gather(head_weight, "dp", axis=0, tiled=True)
    vocab_dev = weight.shape[1]
    own_rows = tensor_idx * row_dev + jnp.arange(row_dev, dtype=jnp.int32)
    logits = jnp.dot(
        lax.all_gather(normed, "tensor", axis=0, tiled=True),
        weight,
        preferred_element_type=jnp.float32,
    )
    top = jnp.max(logits, axis=1)
    expo = jnp.exp(logits - top[:, None])
    total = jnp.sum(expo, axis=1)
    moment = jnp.sum(expo * logits, axis=1)
    ids = lax.all_gather(token_ids, "tensor", axis=0, tiled=True) - tensor_idx * vocab_dev
    hit = ids[:, None] == jnp.arange(vocab_dev, dtype=jnp.int32)[None, :]
    chosen = jnp.sum(jnp.where(hit, logits, 0.0), axis=1)
    seq_iota = jnp.arange(SEQ_DP, dtype=jnp.int32)
    onehot = (own_rows // SLOT)[:, None] == seq_iota[None, :]
    length_of = jnp.sum(jnp.where(onehot, lengths[0][None, :], 0), axis=1)
    scored = own_rows % SLOT < length_of
    top_all = lax.pmax(top, "tensor")
    rescale = jnp.exp(top - top_all)
    total_all, moment_all, chosen_all = lax.psum(
        (total * rescale, moment * rescale, chosen), "tensor"
    )
    return finish(
        scored, top_all[own_rows], total_all[own_rows], moment_all[own_rows], chosen_all[own_rows]
    )


def finish(scored, top, total, moment, chosen):
    safe_total = jnp.where(scored, total, 1.0)
    lse = top + jnp.log(safe_total)
    logprob = jnp.where(scored, chosen - lse, 0.0)
    entropy = jnp.where(scored, lse - moment / safe_total, 0.0)
    return (logprob, entropy)


def head_kernel(
    n_dp, n_z, groups, x_ref, sel_ref, keep_ref, w_ref, out_ref,
    rows, weight, back, front, buf_a, buf_b, acc, stats, dp_parts, part, all_parts,
    plane_send, plane_recv, up_send, up_recv, down_send, down_recv,
    sib_send, sib_recv, w_send, w_recv, local_sem,
    bup_send, bup_recv, bdown_send, bdown_recv, bsib_send, bsib_recv,
    front_send, front_recv, sdp_send, sdp_recv, st_send, st_recv,
    ids_dp, ids_all, idp_send, idp_recv, it_send, it_recv,
):
    dp = lax.axis_index("dp")
    t = lax.axis_index("tensor")
    z, core = t // 2, t % 2
    n_tensor = 2 * n_z
    depth = w_ref.shape[0]
    width, vocab = weight.shape
    share, wide = front.shape
    block = n_dp * share
    sibling = (dp, z * 2 + 1 - core)
    above, below = (dp, t + 2), (dp, t - 2)

    barrier = pltpu.get_barrier_semaphore()
    for k in range(1, n_dp):
        pl.semaphore_signal(barrier, device_id=((dp + k) % n_dp, t), device_id_type=MESH)
    for k in range(1, n_tensor):
        pl.semaphore_signal(barrier, device_id=(dp, (t + k) % n_tensor), device_id_type=MESH)
    pl.semaphore_wait(barrier, n_dp + n_tensor - 2)

    def remote(src, dst, send, recv, to):
        return pltpu.make_async_remote_copy(
            src_ref=src, dst_ref=dst, send_sem=send, recv_sem=recv,
            device_id=to, device_id_type=MESH,
        )

    def back_up(d):
        src = x_ref if d == 0 else back.at[z - d]
        return remote(src, back.at[z - d], bup_send.at[d], bup_recv.at[d], above)

    def back_down(d):
        src = x_ref if d == 0 else back.at[z + d]
        return remote(src, back.at[z + d], bdown_send.at[d], bdown_recv.at[d], below)

    def back_sib(plane):
        return remote(
            back.at[plane], back.at[plane], bsib_send.at[plane], bsib_recv.at[plane], sibling
        )

    front_copy = remote(x_ref.at[share : 2 * share], front, front_send, front_recv, sibling)
    own_front = pltpu.make_async_copy(x_ref.at[0:share], front, local_sem.at[0])

    @pl.when((core == 1) & (z < n_z - 1))
    def _():
        back_up(0).start()

    @pl.when((core == 1) & (z > 0))
    def _():
        back_down(0).start()

    @pl.when(core == 0)
    def _():
        front_copy.start()
        own_front.start()

    def weight_copy(g, k, sender):
        at, size = groups[g][0], sum(groups[g][1])
        peer = (dp + k) % n_dp
        return remote(
            w_ref.at[:, pl.ds(pl.multiple_of(peer * vocab + at, 128), size)],
            weight.at[pl.ds(pl.multiple_of(sender * depth, depth), depth), at : at + size],
            w_send.at[g, k - 1], w_recv.at[g, k - 1], (peer, t),
        )

    for k in range(1, n_dp):
        weight_copy(0, k, dp).start()
    own_weight = pltpu.make_async_copy(
        w_ref.at[:, pl.ds(pl.multiple_of(dp * vocab, 128), vocab)],
        weight.at[pl.ds(pl.multiple_of(dp * depth, depth), depth)],
        local_sem.at[1],
    )
    own_weight.start()

    for d in range(1, n_z):
        @pl.when((core == 1) & (z >= d))
        def _():
            remote(
                back.at[z - d], back.at[z - d], bup_send.at[d - 1], bup_recv.at[d - 1], above
            ).wait_recv()

            @pl.when(z < n_z - 1)
            def _():
                back_up(d).start()

            back_sib(z - d).start()

        @pl.when((core == 1) & (z + d < n_z))
        def _():
            remote(
                back.at[z + d], back.at[z + d], bdown_send.at[d - 1], bdown_recv.at[d - 1], below
            ).wait_recv()

            @pl.when(z > 0)
            def _():
                back_down(d).start()

            back_sib(z + d).start()

    @pl.when(core == 0)
    def _():
        own_front.wait()
        for k in range(1, n_z):
            back_sib((z + k) % n_z).wait_recv()

    @pl.when(core == 1)
    def _():
        front_copy.wait_recv()

    own_at = pl.ds(pl.multiple_of(dp * share, share), share)
    for at in range(0, wide, 512):
        cols = slice(at, min(at + 512, wide))
        mine = front[:, cols].astype(jnp.float32) * keep_ref[:, :1]
        for k in range(1, n_z):
            plane = (z + k) % n_z
            mine += jnp.dot(
                sel_ref[plane], back[plane, :, cols], preferred_element_type=jnp.float32
            )
        if at < width:
            rows[z, core, own_at, cols] = mine.astype(jnp.bfloat16)
            continue
        lane = lax.broadcasted_iota(jnp.int32, (1, 128), 1)
        worth = jnp.where(
            lane == 0, 4096.0, jnp.where(lane == 1, 64.0, jnp.where(lane == 2, 1.0, 0.0))
        )
        ids = jnp.sum(mine * worth, axis=1, keepdims=True)
        ids_dp[dp] = jnp.broadcast_to(ids, (share, 128)).T[:8]

    def ids_dp_copy(k, sender):
        return remote(
            ids_dp.at[sender], ids_dp.at[sender],
            idp_send.at[k - 1], idp_recv.at[k - 1], ((dp + k) % n_dp, t),
        )

    def ids_t_copy(k, sender):
        return remote(
            ids_dp, ids_all.at[sender],
            it_send.at[k - 1], it_recv.at[k - 1], (dp, (t + k) % n_tensor),
        )

    for k in range(1, n_dp):
        ids_dp_copy(k, dp).start()

    def plane_copy(k, sender):
        at = pl.ds(pl.multiple_of(sender * share, share), share)
        return remote(
            rows.at[z, core, at], rows.at[z, core, at],
            plane_send.at[k - 1], plane_recv.at[k - 1], ((dp + k) % n_dp, t),
        )

    for k in range(1, n_dp):
        plane_copy(k, dp).start()
    for g in range(1, len(groups)):
        for k in range(1, n_dp):
            weight_copy(g, k, dp).start()

    def share_of(plane, k):
        at = pl.multiple_of((dp - k + n_dp) % n_dp * share, share)
        return rows.at[plane, core, pl.ds(at, share)]

    def up_copy(d, k, plane):
        ref = share_of(plane, k)
        return remote(ref, ref, up_send.at[d, k], up_recv.at[d, k], above)

    def down_copy(d, k, plane):
        ref = share_of(plane, k)
        return remote(ref, ref, down_send.at[d, k], down_recv.at[d, k], below)

    def sib_copy(plane, half):
        ref = rows.at[plane, half]
        return remote(ref, ref, sib_send.at[plane], sib_recv.at[plane], sibling)

    for k in range(n_dp):
        if k == 1:
            for other in range(1, n_dp):
                ids_dp_copy(other, (dp - other + n_dp) % n_dp).wait_recv()
            for other in range(1, n_tensor):
                ids_t_copy(other, t).start()
            ids_all[t] = ids_dp[...]
        if k:
            plane_copy(k, (dp - k + n_dp) % n_dp).wait_recv()

        @pl.when(z < n_z - 1)
        def _():
            up_copy(0, k, z).start()

        @pl.when(z > 0)
        def _():
            down_copy(0, k, z).start()

    sib_copy(z, core).start()

    def stage(d):
        for k in range(n_dp):
            @pl.when(z >= d)
            def _():
                up_copy(d - 1, k, z - d).wait_recv()

                @pl.when(z < n_z - 1)
                def _():
                    up_copy(d, k, z - d).start()

            @pl.when(z + d < n_z)
            def _():
                down_copy(d - 1, k, z + d).wait_recv()

                @pl.when(z > 0)
                def _():
                    down_copy(d, k, z + d).start()

        @pl.when(z >= d)
        def _():
            sib_copy(z - d, core).start()

        @pl.when(z + d < n_z)
        def _():
            sib_copy(z + d, core).start()

    def wait_weights(g):
        for k in range(1, n_dp):
            weight_copy(g, k, (dp - k + n_dp) % n_dp).wait_recv()

    stage(1)
    own_weight.wait()
    wait_weights(0)
    for k in range(1, n_tensor):
        ids_t_copy(k, (t - k + n_tensor) % n_tensor).wait_recv()

    first = t * (n_dp * vocab) + dp * vocab
    lane = lax.broadcasted_iota(jnp.int32, (1, 128), 1)
    strip = 16

    def multiply(plane, half, g):
        entry = plane * 2 + half
        shifted = []
        for i in range(n_dp):
            ids = jnp.broadcast_to(ids_all[entry, i, 0:1], (128, share)).T
            shifted.append(ids.astype(jnp.int32) - first - lane)
        lhs = rows[plane, half]
        at, sizes = groups[g]
        for i, size in enumerate(sizes):
            buf = (buf_a, buf_b)[i % 2]
            buf[:, :size] = jnp.dot(
                lhs, weight[:, at : at + size], preferred_element_type=jnp.float32
            )
            for r in range(0, block, strip):
                rs = slice(r, r + strip)
                ids = shifted[r // share][r % share : r % share + strip]
                tiles = [buf[rs, c : c + 128] for c in range(0, size, 128)]
                old = acc[entry, 0, rs]
                top = old
                for tile in tiles:
                    top = jnp.maximum(top, tile)
                scale = jnp.exp(old - top)
                total = acc[entry, 1, rs] * scale
                moment = acc[entry, 2, rs] * scale
                chosen = acc[entry, 3, rs]
                for n, tile in enumerate(tiles):
                    e = jnp.exp(tile - top)
                    total += e
                    moment += e * tile
                    chosen += jnp.where(ids == at + n * 128, tile, 0.0)
                acc[entry, 0, rs] = top
                acc[entry, 1, rs] = total
                acc[entry, 2, rs] = moment
                acc[entry, 3, rs] = chosen
            at += size

    near = n_z - 1
    last = len(groups) - 1

    @pl.loop(0, 2 * len(groups) * n_z)
    def _(it):
        unit, turn = it // 2, it % 2
        half = (core + turn) % 2
        far = unit >= near * len(groups)
        group = jnp.where(far, unit - near * len(groups), unit // near)
        order = jnp.where(far, near, unit % near)
        plane = jnp.where(z < n_z // 2, order, n_z - 1 - order)
        entry = plane * 2 + half

        @pl.when(it == 4)
        def _():
            stage(2)

        for g in range(1, len(groups)):
            @pl.when(it == 2 * near * g)
            def _():
                wait_weights(g)

        @pl.when(it == 2 * near * len(groups))
        def _():
            stage(3)

        @pl.when(group == 0)
        def _():
            @pl.when(turn == 1)
            def _():
                sib_copy(plane, 1 - core).wait_recv()

            acc[entry, 0] = jnp.full((block, 128), -3e38, jnp.float32)
            for i in range(1, 4):
                acc[entry, i] = jnp.zeros((block, 128), jnp.float32)

        for g in range(len(groups)):
            @pl.when(group == g)
            def _():
                multiply(plane, half, g)

        @pl.when(group == last)
        def _():
            lanes = acc[entry, 0]
            top = jnp.max(lanes, axis=1, keepdims=True)
            scale = jnp.exp(lanes - top)
            total = jnp.sum(acc[entry, 1] * scale, axis=1, keepdims=True)
            moment = jnp.sum(acc[entry, 2] * scale, axis=1, keepdims=True)
            chosen = jnp.sum(acc[entry, 3], axis=1, keepdims=True)
            packed = jnp.where(
                lane == 0, top, jnp.where(lane == 1, total, jnp.where(lane == 2, moment, chosen))
            )
            stats[entry] = packed.T[:8]

    def merge(parts, n):
        each = [parts[i] for i in range(n)]
        top = each[0][:, 0:1]
        for p in each[1:]:
            top = jnp.maximum(top, p[:, 0:1])
        total = moment = chosen = jnp.zeros_like(top)
        for p in each:
            scale = jnp.exp(p[:, 0:1] - top)
            total += p[:, 1:2] * scale
            moment += p[:, 2:3] * scale
            chosen += p[:, 3:4]
        return jnp.concatenate([top, total, moment, chosen] * 2, axis=1)

    def stats_dp(k, sender):
        peer = (dp + k) % n_dp
        return remote(
            stats.at[:, :, pl.ds(pl.multiple_of(peer * share, share), share)], dp_parts.at[sender],
            sdp_send.at[k - 1], sdp_recv.at[k - 1], (peer, t),
        )

    for k in range(1, n_dp):
        stats_dp(k, dp).start()
    own_stats = pltpu.make_async_copy(
        stats.at[:, :, pl.ds(pl.multiple_of(dp * share, share), share)], dp_parts.at[dp], local_sem.at[2]
    )
    own_stats.start()
    own_stats.wait()
    for k in range(1, n_dp):
        stats_dp(k, (dp - k + n_dp) % n_dp).wait_recv()
    part[...] = merge(dp_parts, n_dp)

    def stats_t(k, sender):
        return remote(
            part, all_parts.at[sender], st_send.at[k - 1], st_recv.at[k - 1],
            (dp, (t + k) % n_tensor),
        )

    for k in range(1, n_tensor):
        stats_t(k, t).start()
    all_parts[t] = part[...]
    for k in range(1, n_tensor):
        stats_t(k, (t - k + n_tensor) % n_tensor).wait_recv()
    out_ref[...] = merge(all_parts, n_tensor)

    for k in range(1, n_dp):
        plane_copy(k, dp).wait_send()
        ids_dp_copy(k, dp).wait_send()
        stats_dp(k, dp).wait_send()
        for g in range(len(groups)):
            weight_copy(g, k, dp).wait_send()
    for k in range(1, n_tensor):
        stats_t(k, t).wait_send()
        ids_t_copy(k, t).wait_send()
    for plane in range(n_z):
        sib_copy(plane, core).wait_send()

    @pl.when(core == 0)
    def _():
        front_copy.wait_send()

    @pl.when(core == 1)
    def _():
        for k in range(1, n_z):
            back_sib((z + k) % n_z).wait_send()

    for d in range(n_z - 1):
        @pl.when((z >= d) & (z < n_z - 1))
        def _():
            for k in range(n_dp):
                up_copy(d, k, z - d).wait_send()

            @pl.when(core == 1)
            def _():
                back_up(d).wait_send()

        @pl.when((z + d < n_z) & (z > 0))
        def _():
            for k in range(n_dp):
                down_copy(d, k, z + d).wait_send()

            @pl.when(core == 1)
            def _():
                back_down(d).wait_send()


def split_columns(vocab):
    parts = [vocab * share // 25 // 128 * 128 for share in (6, 8, 7)]
    return parts + [vocab - sum(parts)]


def head_stats(n_dp, n_z, sent, select, keep, head_weight):
    wide = sent.shape[1]
    share = sent.shape[0] // 2
    depth, vocab_dev = head_weight.shape
    width, vocab, block = n_dp * depth, vocab_dev // n_dp, n_dp * share
    groups, at = [], 0
    for part in split_columns(vocab):
        sizes = [min(512, part - done) for done in range(0, part, 512)]
        groups.append((at, sizes))
        at += part
    dma = pltpu.SemaphoreType.DMA
    n_tensor = 2 * n_z
    f32, bf16 = jnp.float32, jnp.bfloat16
    vmem = pl.BlockSpec(memory_space=pltpu.VMEM)
    return pl.pallas_call(
        functools.partial(head_kernel, n_dp, n_z, groups),
        out_shape=jax.ShapeDtypeStruct((n_tensor, 8, share), f32),
        in_specs=[vmem, vmem, vmem, pl.BlockSpec(memory_space=pl.ANY)],
        out_specs=vmem,
        scratch_shapes=[
            pltpu.VMEM((n_z, 2, block, width), bf16),
            pltpu.VMEM((width, vocab), bf16),
            pltpu.VMEM((n_z, 2 * share, wide), bf16),
            pltpu.VMEM((share, wide), bf16),
            pltpu.VMEM((block, 512), f32),
            pltpu.VMEM((block, 512), f32),
            pltpu.VMEM((n_tensor, 4, block, 128), f32),
            pltpu.VMEM((n_tensor, 8, block), f32),
            pltpu.VMEM((n_dp, n_tensor, 8, share), f32),
            pltpu.VMEM((n_tensor, 8, share), f32),
            pltpu.VMEM((n_tensor, n_tensor, 8, share), f32),
            dma((n_dp - 1,)), dma((n_dp - 1,)),
            dma((n_z, n_dp)), dma((n_z, n_dp)), dma((n_z, n_dp)), dma((n_z, n_dp)),
            dma((n_z,)), dma((n_z,)),
            dma((len(groups), n_dp - 1)), dma((len(groups), n_dp - 1)),
            dma((3,)),
            dma((n_z,)), dma((n_z,)), dma((n_z,)), dma((n_z,)),
            dma((n_z,)), dma((n_z,)),
            dma, dma,
            dma((n_dp - 1,)), dma((n_dp - 1,)),
            dma((n_tensor - 1,)), dma((n_tensor - 1,)),
            pltpu.VMEM((n_dp, 8, share), f32),
            pltpu.VMEM((n_tensor, n_dp, 8, share), f32),
            dma((n_dp - 1,)), dma((n_dp - 1,)),
            dma((n_tensor - 1,)), dma((n_tensor - 1,)),
        ],
        compiler_params=pltpu.CompilerParams(
            collective_id=0, has_side_effects=True, vmem_limit_bytes=60 * 1024 * 1024
        ),
        cost_estimate=pl.CostEstimate(
            flops=2 * n_tensor * block * width * vocab,
            bytes_accessed=width * vocab * 2,
            transcendentals=n_tensor * block * vocab,
        ),
    )(sent, select, keep, head_weight)


def last_at_or_below(starts, value):
    return jnp.sum((value[:, None] >= starts[None, :]).astype(jnp.int32), axis=1) - 1


def pick(table, index):
    iota = jnp.arange(table.shape[0], dtype=jnp.int32)
    return jnp.sum(jnp.where(index[:, None] == iota[None, :], table[None, :], 0), axis=1)


def kernel_device(n_dp, n_tensor, hidden, norm_gain, head_weight, token_ids, lengths):
    row_dev = hidden.shape[0]
    n_z = n_tensor // 2
    t = lax.axis_index("tensor")
    z, core = t // 2, t % 2
    length = lengths[0]
    over = jnp.maximum(length - row_dev, 0)
    under = jnp.maximum(row_dev - length, 0)
    over_at = jnp.cumsum(over) - over
    under_at = jnp.cumsum(under) - under

    normed = normalize(hidden, norm_gain)
    lane = jnp.arange(TAIL, dtype=jnp.int32)[None, :]
    ids = token_ids[:, None]
    digits = jnp.where(
        lane == 0, ids // 4096, jnp.where(lane == 1, ids // 64 % 64, jnp.where(lane == 2, ids % 64, 0))
    )
    sent = jnp.concatenate([normed, digits.astype(jnp.bfloat16)], axis=1)

    share = row_dev // 2
    slot = t * share + jnp.arange(share, dtype=jnp.int32)
    place = slot % row_dev
    zs = jnp.full((share,), z, jnp.int32)
    own_len = pick(length, zs)
    extra = pick(under_at, zs) + place - own_len
    giver = last_at_or_below(over_at, extra)
    from_back = extra - pick(over_at, giver)
    filled = (place >= own_len)[None, :] & (giver[None, :] == jnp.arange(n_z, dtype=jnp.int32)[:, None])
    row_iota = jnp.arange(row_dev, dtype=jnp.int32)
    select = filled[:, :, None] & (from_back[:, None] == row_iota[None, :])[None]
    select = select.astype(jnp.bfloat16)
    keep = jnp.broadcast_to((place < own_len)[:, None], (share, 128)).astype(jnp.float32)
    full = head_stats(n_dp, n_z, sent, select, keep, head_weight)
    full = full[:, :4].transpose(1, 0, 2).reshape(4, -1)

    row = jnp.arange(row_dev, dtype=jnp.int32)
    zr = jnp.full((row_dev,), z, jnp.int32)
    extra = pick(over_at, zr) + row
    taker = last_at_or_below(under_at, extra)
    back = taker * row_dev + pick(length, taker) + extra - pick(under_at, taker)
    where = jnp.where(core == 0, z * row_dev + row, back)
    scored = core * row_dev + row < pick(length, zr)
    hit = where[:, None] == jnp.arange(n_tensor * share, dtype=jnp.int32)[None, :]
    own = [jnp.sum(jnp.where(hit, full[i][None, :], 0.0), axis=1) for i in range(4)]
    return finish(scored, *own)


def solution(mesh):
    n_dp, n_tensor = mesh.shape["dp"], mesh.shape["tensor"]

    def per_device(hidden, norm_gain, head_weight, token_ids, lengths):
        fits = (
            n_tensor == 2 * SEQ_DP
            and 2 * hidden.shape[0] == SLOT
            and head_weight.shape[1] % (128 * n_dp) == 0
        )
        if not fits:
            return plain_device(hidden, norm_gain, head_weight, token_ids, lengths)
        return kernel_device(n_dp, n_tensor, hidden, norm_gain, head_weight, token_ids, lengths)

    return jax.shard_map(
        per_device,
        mesh=mesh,
        in_specs=(
            P(("dp", "tensor"), None),
            P(),
            P("dp", "tensor"),
            P(("dp", "tensor")),
            P("dp", None),
        ),
        out_specs=(P(("dp", "tensor")), P(("dp", "tensor"))),
        check_vma=False,
    )
```
